512 devices in a mesh: grp: 16 (over y, x), dev: 32 (over z, core).
Axes of the slice: x: 4, y: 4, z: 16, core: 2. Of those that a mesh axis runs over, the one named last changes fastest.
Arguments:
- positions: float32 [3, 524288], P(None, ('grp', 'dev')), may hold values from -6 to 6
- velocities: float32 [3, 524288], P(None, ('grp', 'dev')), may hold values from -6 to 6
- masses: float32 [524288], P(('grp', 'dev')), may hold values from 0.2 to 5
- active_index: int32 [1024], replicated, may hold values from 0 to 524287, as said below
Outputs:
- force: float32 [3, 1024], P(None, ('grp', 'dev'))
- jerk: float32 [3, 1024], P(None, ('grp', 'dev'))
The draws below stay inside these ranges and needn't reach their ends.
Inputs may be any that keep to these rules, and one draw needn't show every extreme that they name: `active_index`: strictly increasing, distinct indices of stars; at most 4 of them fall in any aligned block of 1024 consecutive stars, and some block holds exactly 4.
All inputs are finite; a program needn't handle non-finite values.
Results may differ from the reference program's by a relative error of at most 0.0003.
Values sent between devices are 32-bit elements; how exact they have to be, the bound alone decides.
No kernel may reach another device: no remote copies, remote signals or barrier semaphores. Data moves between devices by JAX's collectives and lax.ppermute only.
A program may use at most 64 MiB of HBM per device.

```python
import math
import jax
import jax.numpy as jnp
from jax import lax

STARS_DEV = 1024
ACTIVE = 1024
STARS = 524288


def draw_active_index(key, part):
    ndev = STARS // STARS_DEV
    mean = ACTIVE // ndev
    pattern = jnp.tile(jnp.array([2, 1, 1, 0], jnp.int32) * mean, ndev // 4)
    order_dev = jax.random.permutation(jax.random.fold_in(key, 11), ndev)
    counts = pattern[order_dev]
    top = max(2, 2 ** 30 // STARS_DEV)
    scores = jax.random.randint(jax.random.fold_in(key, 13), (ndev, STARS_DEV), 0, top, dtype=jnp.int32)
    scores = scores * STARS_DEV + jnp.arange(STARS_DEV, dtype=jnp.int32)[None, :]
    order = jnp.argsort(scores, axis=1)
    ranks = jnp.argsort(order, axis=1)
    chosen = (ranks < counts[:, None]).reshape(-1)
    picked = jnp.nonzero(chosen, size=ACTIVE, fill_value=0)[0]
    return picked.astype(jnp.int32)


def shard_levels(key, extent, cuts, smallest, top_value):
    gain = 1.0
    for axis_at, shards_of in cuts:
        draws = jax.random.uniform(jax.random.fold_in(jax.random.fold_in(key, 6), axis_at), (shards_of,), jnp.float32, smallest / len(cuts), top_value / len(cuts))
        gain = gain * jnp.repeat(jnp.exp(draws), extent[axis_at] // shards_of).reshape((-1,) + (1,) * (len(extent) - 1 - axis_at))
    return gain


def normal_values(rng, shape, spread, reach, cuts=(), kind=jnp.bfloat16):
    level = shard_levels(rng, shape, cuts, -0.22, 0.18) if cuts else 1.0
    values = jax.random.normal(rng, shape, jnp.float32) * spread * level
    return jnp.minimum(jnp.maximum(values, -reach), reach).astype(kind)


def setup_inputs(seed: int = 0) -> dict:
    seeds = jax.random.split(jax.random.key(seed), 5)
    positions = normal_values(seeds[0], (3, STARS), 1.0, 6.0, ((1, 512),), jnp.float32)
    velocities = normal_values(seeds[1], (3, STARS), 1.0, 6.0, ((1, 512),), jnp.float32)
    masses = jnp.clip(jnp.exp(math.log(5.0) - 3.218876 * jax.random.uniform(seeds[2], (STARS,), jnp.float32) ** shard_levels(seeds[2], (STARS,), ((0, 512),), -0.2, 0.2)), 0.2, 5.0)
    active_index = draw_active_index(jax.random.fold_in(seeds[4], 71), 0)
    return dict(positions=positions, velocities=velocities, masses=masses, active_index=active_index)


SOFT = 0.0025

def pair_terms(act_pos, act_vel, pos, vel, mass):
    dx = pos[:, None, :] - act_pos[:, :, None]
    dv = vel[:, None, :] - act_vel[:, :, None]
    r2 = lax.optimization_barrier(jnp.sum(dx * dx, axis=0)) + SOFT
    inv = 1.0 / jnp.sqrt(r2)
    weight = mass[None, :] * inv * inv * inv
    rv = lax.optimization_barrier(jnp.sum(dx * dv, axis=0))
    acc = lax.optimization_barrier(jnp.sum(weight[None] * dx, axis=-1))
    jer = lax.optimization_barrier(jnp.sum(weight[None] * dv - (3.0 * rv * weight / r2)[None] * dx, axis=-1))
    return (acc, jer)

def reference(positions, velocities, masses, active_index):
    block = min(256, ACTIVE)
    star_block = min(16384, STARS)
    act_pos = jnp.take(positions, active_index, axis=1)
    act_vel = jnp.take(velocities, active_index, axis=1)
    nblk = ACTIVE // block
    nstar = STARS // star_block
    apos = act_pos.reshape(3, nblk, block).transpose(1, 0, 2)
    avel = act_vel.reshape(3, nblk, block).transpose(1, 0, 2)
    spos = positions.reshape(3, nstar, star_block).transpose(1, 0, 2)
    svel = velocities.reshape(3, nstar, star_block).transpose(1, 0, 2)
    smass = masses.reshape(nstar, star_block)

    def one_block(item):
        bpos, bvel = item

        def step(carry, piece):
            acc, jer = pair_terms(bpos, bvel, piece[0], piece[1], piece[2])
            return ((carry[0] + acc, carry[1] + jer), None)
        zeros = jnp.zeros((3, block), jnp.float32)
        (acc, jer), _ = lax.scan(step, (zeros, zeros), (spos, svel, smass))
        return (acc, jer)
    acc, jer = lax.map(one_block, (apos, avel))
    scale = 1.0 / STARS
    force = acc.transpose(1, 0, 2).reshape(3, ACTIVE) * scale
    jerk = jer.transpose(1, 0, 2).reshape(3, ACTIVE) * scale
    return (force, jerk)
```

```python
import jax
import jax.numpy as jnp
from jax import lax
from jax.experimental import pallas as pl
from jax.experimental.pallas import tpu as pltpu
from jax.sharding import PartitionSpec as P

SOFT = 0.0025
LANES = 128
WHOLE = pl.BlockSpec(memory_space=pltpu.VMEM)
SCALARS = pl.BlockSpec(memory_space=pltpu.SMEM)


def pack_kernel(index_ref, pos_ref, vel_ref, mass_ref, out_ref):
    active = index_ref.shape[0]
    count = pos_ref.shape[1]
    groups = out_ref.shape[0]
    per_group = active // groups
    owner = lax.axis_index("grp") * lax.axis_size("dev") + lax.axis_index("dev")
    offset = owner * count
    mass = mass_ref[...]
    rows = jnp.concatenate([pos_ref[...], vel_ref[...], mass, jnp.zeros_like(mass)], axis=0)
    for g in range(groups):
        out_ref[g] = rows
    first = jnp.int32(0)
    step = active // 2
    while step:
        first = first + jnp.where(index_ref[first + (step - 1)] < offset, step, 0)
        step //= 2
    first = first + jnp.where(index_ref[first] < offset, 1, 0)
    lane = lax.broadcasted_iota(jnp.int32, (3, LANES), 1)
    for k in range(4):
        rank = jnp.minimum(first + k, active - 1)
        local = index_ref[rank] - offset

        @pl.when((first + k < active) & (local < count))
        def _():
            chunk = pl.ds(pl.multiple_of(local // LANES * LANES, LANES), LANES)
            here = lane == local % LANES
            pos = jnp.sum(jnp.where(here, pos_ref[:, chunk], 0.0), axis=1, keepdims=True)
            vel = jnp.sum(jnp.where(here, vel_ref[:, chunk], 0.0), axis=1, keepdims=True)
            group = rank // per_group
            slot = rank % per_group
            state = jnp.where(lane == slot, pos, jnp.where(lane == slot + LANES // 2, vel, 0.0))
            for c in range(3):
                tile = pl.ds(c * LANES, LANES)
                out_ref[group, 7:8, tile] = out_ref[group, 7:8, tile] + state[c : c + 1]


def spread_kernel(in_ref, out_ref):
    for c in range(3):
        tile = pl.ds(c * LANES, LANES)
        total = in_ref[0, 7:8, tile]
        for g in range(1, in_ref.shape[0]):
            total = total + in_ref[g, 7:8, tile]
        for d in range(out_ref.shape[0]):
            out_ref[d, c] = total


def pairs_kernel(state_ref, field_ref, out_ref):
    sources, _, count = field_ref.shape
    width = 4
    rows = []
    for c in range(3):
        total = state_ref[0, c]
        for d in range(1, state_ref.shape[0]):
            total = total + state_ref[d, c]
        rows.append(total)
    packed = jnp.concatenate(rows + [jnp.zeros((5, LANES), jnp.float32)], axis=0).T
    lane = lax.broadcasted_iota(jnp.int32, (8, LANES), 1)
    half = LANES // 2
    zero = jnp.zeros((8, LANES), jnp.float32)
    for top in range(0, half // 8, width):
        states = [
            [
                jnp.broadcast_to(packed[h + 8 * (top + i) : h + 8 * (top + i) + 8, c : c + 1], (8, LANES))
                for h in (0, half)
                for c in range(3)
            ]
            for i in range(width)
        ]

        def one_source(b, sums, states=states):
            sums = [list(s) for s in sums]
            for t in range(0, count, LANES):
                star = [jnp.broadcast_to(field_ref[b, c : c + 1, t : t + LANES], (8, LANES)) for c in range(7)]
                for act, s in zip(states, sums):
                    dx = [star[c] - act[c] for c in range(3)]
                    dv = [star[3 + c] - act[3 + c] for c in range(3)]
                    r2 = dx[0] * dx[0] + dx[1] * dx[1] + dx[2] * dx[2] + SOFT
                    inv = lax.rsqrt(r2)
                    rv = dx[0] * dv[0] + dx[1] * dv[1] + dx[2] * dv[2]
                    inv2 = inv * inv
                    weight = star[6] * inv * inv2
                    ratio = rv * inv2
                    for c in range(3):
                        pull = weight * dx[c]
                        s[c] = s[c] + pull
                        s[3 + c] = s[3 + c] + weight * dv[c]
                        s[6 + c] = s[6 + c] + ratio * pull
            return tuple(tuple(s) for s in sums)

        sums = lax.fori_loop(0, sources, one_source, ((zero,) * 9,) * width)
        for i, s in enumerate(sums):
            result = zero
            for c in range(3):
                force = jnp.sum(s[c], axis=1, keepdims=True)
                jerk = jnp.sum(s[3 + c] - 3.0 * s[6 + c], axis=1, keepdims=True)
                result = jnp.where(lane == c, force, jnp.where(lane == 3 + c, jerk, result))
            out_ref[pl.ds(8 * (top + i), 8), 0, :] = result


def finish_kernel(scale, in_ref, force_ref, jerk_ref):
    slots = force_ref.shape[0]
    rows = []
    for i in range(slots):
        total = in_ref[i]
        for d in range(1, in_ref.shape[0] // slots):
            total = total + in_ref[d * slots + i]
        rows.append(total)
    rows.append(jnp.zeros((8 - slots, LANES), jnp.float32))
    total = jnp.concatenate(rows, axis=0) * scale
    force_ref[...] = total[0:slots, 0:3]
    jerk_ref[...] = total[0:slots, 3:6]


def per_device(positions, velocities, masses, active_index):
    groups, members = lax.axis_size("grp"), lax.axis_size("dev")
    count = positions.shape[1]
    active = active_index.shape[0]
    f32 = jnp.float32
    packed = pl.pallas_call(
        pack_kernel,
        out_shape=jax.ShapeDtypeStruct((groups, 8, count), f32),
        in_specs=[SCALARS, WHOLE, WHOLE, WHOLE],
        out_specs=WHOLE,
        name="pack",
    )(active_index, positions, velocities, masses.reshape(1, count))
    field = lax.all_to_all(packed, "grp", 0, 0, tiled=True)
    spread = pl.pallas_call(
        spread_kernel,
        out_shape=jax.ShapeDtypeStruct((members, 3, 1, LANES), f32),
        grid=(1,),
        in_specs=[pl.BlockSpec((groups, 8, 3 * LANES), lambda i: (0, 0, 0))],
        out_specs=pl.BlockSpec((members, 3, 1, LANES), lambda i: (0, 0, 0, 0)),
        name="spread",
    )(field)
    states = lax.all_to_all(spread, "dev", 0, 0, tiled=True)
    per_group = active // groups
    partial = pl.pallas_call(
        pairs_kernel,
        out_shape=jax.ShapeDtypeStruct((per_group, 1, LANES), f32),
        in_specs=[WHOLE, WHOLE],
        out_specs=WHOLE,
        name="pairs",
    )(states, field)
    arrived = lax.all_to_all(partial, "dev", 0, 0, tiled=True)
    slots = per_group // members
    out = jax.ShapeDtypeStruct((slots, 3), f32)
    scale = 1.0 / (count * groups * members)
    force, jerk = pl.pallas_call(
        lambda *refs: finish_kernel(scale, *refs),
        out_shape=(out, out),
        in_specs=[WHOLE],
        out_specs=(WHOLE, WHOLE),
        name="finish",
    )(arrived)
    return force.T, jerk.T


def solution(mesh):
    both = ("grp", "dev")
    return jax.shard_map(
        per_device,
        mesh=mesh,
        in_specs=(P(None, both), P(None, both), P(both), P()),
        out_specs=(P(None, both), P(None, both)),
        check_vma=False,
    )
```

```python
import jax
import jax.numpy as jnp
from jax import lax
from jax.experimental import pallas as pl
from jax.experimental.pallas import tpu as pltpu
from jax.sharding import PartitionSpec as P

SOFT = 0.0025
LANES = 128
WHOLE = pl.BlockSpec(memory_space=pltpu.VMEM)
SCALARS = pl.BlockSpec(memory_space=pltpu.SMEM)


def pack_kernel(index_ref, pos_ref, vel_ref, mass_ref, out_ref):
    active = index_ref.shape[0]
    count = pos_ref.shape[1]
    groups = out_ref.shape[0]
    per_group = active // groups
    owner = lax.axis_index("grp") * lax.axis_size("dev") + lax.axis_index("dev")
    offset = owner * count
    mass = mass_ref[...]
    rows = jnp.concatenate([pos_ref[...], vel_ref[...], mass, jnp.zeros_like(mass)], axis=0)
    for g in range(groups):
        out_ref[g] = rows
    first = jnp.int32(0)
    step = active // 2
    while step:
        first = first + jnp.where(index_ref[first + (step - 1)] < offset, step, 0)
        step //= 2
    first = first + jnp.where(index_ref[first] < offset, 1, 0)
    lane = lax.broadcasted_iota(jnp.int32, (3, LANES), 1)
    for k in range(4):
        rank = jnp.minimum(first + k, active - 1)
        local = index_ref[rank] - offset

        @pl.when((first + k < active) & (local < count))
        def _():
            chunk = pl.ds(pl.multiple_of(local // LANES * LANES, LANES), LANES)
            here = lane == local % LANES
            pos = jnp.sum(jnp.where(here, pos_ref[:, chunk], 0.0), axis=1, keepdims=True)
            vel = jnp.sum(jnp.where(here, vel_ref[:, chunk], 0.0), axis=1, keepdims=True)
            group = rank // per_group
            slot = rank % per_group
            slot = slot % 2 * (per_group // 2) + slot // 2
            state = jnp.where(lane == slot, pos, jnp.where(lane == slot + LANES // 2, vel, 0.0))
            for c in range(3):
                tile = pl.ds(c * LANES, LANES)
                out_ref[group, 7:8, tile] = out_ref[group, 7:8, tile] + state[c : c + 1]


def spread_kernel(in_ref, out_ref):
    for c in range(3):
        tile = pl.ds(c * LANES, LANES)
        total = in_ref[0, 7:8, tile]
        for g in range(1, in_ref.shape[0]):
            total = total + in_ref[g, 7:8, tile]
        for d in range(out_ref.shape[0]):
            out_ref[d, c] = total


def pairs_kernel(state_ref, field_ref, out_ref):
    sources, _, count = field_ref.shape
    width = 4
    rows = []
    for c in range(3):
        total = state_ref[0, c]
        for d in range(1, state_ref.shape[0]):
            total = total + state_ref[d, c]
        rows.append(total)
    packed = jnp.concatenate(rows + [jnp.zeros((5, LANES), jnp.float32)], axis=0).T
    lane = lax.broadcasted_iota(jnp.int32, (8, LANES), 1)
    half = LANES // 2
    zero = jnp.zeros((8, LANES), jnp.float32)
    results = []
    for top in range(0, half // 8, width):
        states = [
            [
                jnp.broadcast_to(packed[h + 8 * (top + i) : h + 8 * (top + i) + 8, c : c + 1], (8, LANES))
                for h in (0, half)
                for c in range(3)
            ]
            for i in range(width)
        ]

        def one_source(b, sums, states=states):
            sums = [list(s) for s in sums]
            for t in range(0, count, LANES):
                star = [jnp.broadcast_to(field_ref[b, c : c + 1, t : t + LANES], (8, LANES)) for c in range(7)]
                for act, s in zip(states, sums):
                    dx = [star[c] - act[c] for c in range(3)]
                    dv = [star[3 + c] - act[3 + c] for c in range(3)]
                    r2 = dx[0] * dx[0] + dx[1] * dx[1] + dx[2] * dx[2] + SOFT
                    inv = lax.rsqrt(r2)
                    rv = dx[0] * dv[0] + dx[1] * dv[1] + dx[2] * dv[2]
                    inv2 = inv * inv
                    weight = star[6] * inv * inv2
                    ratio = rv * inv2
                    for c in range(3):
                        pull = weight * dx[c]
                        s[c] = s[c] + pull
                        s[3 + c] = s[3 + c] + weight * dv[c]
                        s[6 + c] = s[6 + c] + ratio * pull
            return tuple(tuple(s) for s in sums)

        sums = lax.fori_loop(0, sources, one_source, ((zero,) * 9,) * width)
        first = 6 * (2 * top // (half // 8))
        for s in sums:
            result = zero
            for c in range(3):
                force = jnp.sum(s[c], axis=1, keepdims=True)
                jerk = jnp.sum(s[3 + c] - 3.0 * s[6 + c], axis=1, keepdims=True)
                result = jnp.where(lane == first + c, force, jnp.where(lane == first + 3 + c, jerk, result))
            results.append(result)
    for i in range(len(results) // 2):
        out_ref[pl.ds(8 * i, 8), 0, :] = results[i] + results[i + len(results) // 2]


def finish_kernel(scale, in_ref, force_ref, jerk_ref):
    total = in_ref[0]
    for d in range(1, in_ref.shape[0]):
        total = total + in_ref[d]
    total = total * scale
    for slot in range(force_ref.shape[0]):
        force_ref[slot : slot + 1, :] = total[:, 6 * slot : 6 * slot + 3]
        jerk_ref[slot : slot + 1, :] = total[:, 6 * slot + 3 : 6 * slot + 6]


def near(x):
    return pltpu.with_memory_space_constraint(x, pltpu.VMEM)


def per_device(positions, velocities, masses, active_index):
    groups, members = lax.axis_size("grp"), lax.axis_size("dev")
    count = positions.shape[1]
    active = active_index.shape[0]
    f32 = jnp.float32
    packed = pl.pallas_call(
        pack_kernel,
        out_shape=pltpu.VMEM((groups, 8, count), f32),
        in_specs=[SCALARS, WHOLE, WHOLE, WHOLE],
        out_specs=WHOLE,
        name="pack",
    )(active_index, positions, velocities, masses.reshape(1, count))
    field = lax.all_to_all(packed, "grp", 0, 0, tiled=True)
    spread = pl.pallas_call(
        spread_kernel,
        out_shape=pltpu.VMEM((members, 3, 1, LANES), f32),
        in_specs=[WHOLE],
        out_specs=WHOLE,
        name="spread",
    )(near(field))
    states = lax.all_to_all(spread, "dev", 0, 0, tiled=True)
    per_group = active // groups
    partial = pl.pallas_call(
        pairs_kernel,
        out_shape=pltpu.VMEM((members, 1, LANES), f32),
        in_specs=[WHOLE, WHOLE],
        out_specs=WHOLE,
        name="pairs",
    )(near(states), near(field))
    arrived = lax.all_to_all(partial, "dev", 0, 0, tiled=True)
    slots = per_group // members
    out = jax.ShapeDtypeStruct((slots, 3), f32)
    scale = 1.0 / (count * groups * members)
    force, jerk = pl.pallas_call(
        lambda *refs: finish_kernel(scale, *refs),
        out_shape=(out, out),
        in_specs=[WHOLE],
        out_specs=(WHOLE, WHOLE),
        name="finish",
    )(near(arrived))
    return force.T, jerk.T


def solution(mesh):
    both = ("grp", "dev")
    return jax.shard_map(
        per_device,
        mesh=mesh,
        in_specs=(P(None, both), P(None, both), P(both), P()),
        out_specs=(P(None, both), P(None, both)),
        check_vma=False,
    )
```

```python
import jax
import jax.numpy as jnp
from jax import lax
from jax.experimental import pallas as pl
from jax.experimental.pallas import tpu as pltpu
from jax.sharding import PartitionSpec as P

SOFT = 0.0025
LANES = 128
GRP_FIRST = 10
DEV_FIRST = 16
WHOLE = pl.BlockSpec(memory_space=pltpu.VMEM)
SCALARS = pl.BlockSpec(memory_space=pltpu.SMEM)


def pack_kernel(index_ref, pos_ref, vel_ref, mass_ref, out_ref):
    active = index_ref.shape[0]
    count = pos_ref.shape[1]
    groups = out_ref.shape[0]
    per_group = active // groups
    owner = lax.axis_index("grp") * lax.axis_size("dev") + lax.axis_index("dev")
    offset = owner * count
    mass = mass_ref[...]
    rows = jnp.concatenate([pos_ref[...], vel_ref[...], mass, jnp.zeros_like(mass)], axis=0)
    for g in range(groups):
        out_ref[g] = rows
    first = jnp.int32(0)
    step = active // 2
    while step:
        first = first + jnp.where(index_ref[first + (step - 1)] < offset, step, 0)
        step //= 2
    first = first + jnp.where(index_ref[first] < offset, 1, 0)
    lane = lax.broadcasted_iota(jnp.int32, (3, LANES), 1)
    for k in range(4):
        rank = jnp.minimum(first + k, active - 1)
        local = index_ref[rank] - offset

        @pl.when((first + k < active) & (local < count))
        def _():
            chunk = pl.ds(pl.multiple_of(local // LANES * LANES, LANES), LANES)
            here = lane == local % LANES
            pos = jnp.sum(jnp.where(here, pos_ref[:, chunk], 0.0), axis=1, keepdims=True)
            vel = jnp.sum(jnp.where(here, vel_ref[:, chunk], 0.0), axis=1, keepdims=True)
            row = (rank // per_group + (groups - GRP_FIRST)) % groups
            slot = rank % per_group
            slot = slot % 2 * (per_group // 2) + slot // 2
            state = jnp.where(lane == slot, pos, jnp.where(lane == slot + LANES // 2, vel, 0.0))
            for c in range(3):
                tile = pl.ds(c * LANES, LANES)
                out_ref[row, 7:8, tile] = out_ref[row, 7:8, tile] + state[c : c + 1]


def spread_kernel(in_ref, out_ref):
    for c in range(3):
        tile = pl.ds(c * LANES, LANES)
        total = in_ref[0, 7:8, tile]
        for g in range(1, in_ref.shape[0]):
            total = total + in_ref[g, 7:8, tile]
        for d in range(out_ref.shape[0]):
            out_ref[d, c] = total


def pairs_kernel(state_ref, field_ref, out_ref):
    sources, _, count = field_ref.shape
    width = 4
    rows = []
    for c in range(3):
        total = state_ref[0, c]
        for d in range(1, state_ref.shape[0]):
            total = total + state_ref[d, c]
        rows.append(total)
    packed = jnp.concatenate(rows + [jnp.zeros((5, LANES), jnp.float32)], axis=0).T
    lane = lax.broadcasted_iota(jnp.int32, (8, LANES), 1)
    half = LANES // 2
    zero = jnp.zeros((8, LANES), jnp.float32)
    results = []
    for top in range(0, half // 8, width):
        states = [
            [
                jnp.broadcast_to(packed[h + 8 * (top + i) : h + 8 * (top + i) + 8, c : c + 1], (8, LANES))
                for h in (0, half)
                for c in range(3)
            ]
            for i in range(width)
        ]

        def one_source(b, sums, states=states):
            sums = [list(s) for s in sums]
            for t in range(0, count, LANES):
                star = [jnp.broadcast_to(field_ref[b, c : c + 1, t : t + LANES], (8, LANES)) for c in range(7)]
                for act, s in zip(states, sums):
                    dx = [star[c] - act[c] for c in range(3)]
                    dv = [star[3 + c] - act[3 + c] for c in range(3)]
                    r2 = dx[0] * dx[0] + dx[1] * dx[1] + dx[2] * dx[2] + SOFT
                    inv = lax.rsqrt(r2)
                    rv = dx[0] * dv[0] + dx[1] * dv[1] + dx[2] * dv[2]
                    inv2 = inv * inv
                    weight = star[6] * inv * inv2
                    ratio = rv * inv2
                    for c in range(3):
                        pull = weight * dx[c]
                        s[c] = s[c] + pull
                        s[3 + c] = s[3 + c] + weight * dv[c]
                        s[6 + c] = s[6 + c] + ratio * pull
            return tuple(tuple(s) for s in sums)

        sums = lax.fori_loop(0, sources, one_source, ((zero,) * 9,) * width)
        first = 6 * (2 * top // (half // 8))
        for s in sums:
            result = zero
            for c in range(3):
                force = jnp.sum(s[c], axis=1, keepdims=True)
                jerk = jnp.sum(s[3 + c] - 3.0 * s[6 + c], axis=1, keepdims=True)
                result = jnp.where(lane == first + c, force, jnp.where(lane == first + 3 + c, jerk, result))
            results.append(result)
    members = out_ref.shape[0]
    for i in range(len(results) // 2):
        row = (8 * i + members - DEV_FIRST) % members
        out_ref[pl.ds(row, 8), 0, :] = results[i] + results[i + len(results) // 2]


def finish_kernel(scale, in_ref, force_ref, jerk_ref):
    total = in_ref[0]
    for d in range(1, in_ref.shape[0]):
        total = total + in_ref[d]
    total = total * scale
    for slot in range(force_ref.shape[0]):
        force_ref[slot : slot + 1, :] = total[:, 6 * slot : 6 * slot + 3]
        jerk_ref[slot : slot + 1, :] = total[:, 6 * slot + 3 : 6 * slot + 6]


def exchanged(x, axis, first):
    count = lax.axis_size(axis)
    order = [(first + m) % count for m in range(count)]
    return lax.all_to_all(x, axis, 0, 0, axis_index_groups=[order], tiled=True)


def near(x):
    return pltpu.with_memory_space_constraint(x, pltpu.VMEM)


def per_device(positions, velocities, masses, active_index):
    groups, members = lax.axis_size("grp"), lax.axis_size("dev")
    count = positions.shape[1]
    active = active_index.shape[0]
    f32 = jnp.float32
    packed = pl.pallas_call(
        pack_kernel,
        out_shape=pltpu.VMEM((groups, 8, count), f32),
        in_specs=[SCALARS, WHOLE, WHOLE, WHOLE],
        out_specs=WHOLE,
        name="pack",
    )(active_index, positions, velocities, masses.reshape(1, count))
    field = exchanged(packed, "grp", GRP_FIRST)
    spread = pl.pallas_call(
        spread_kernel,
        out_shape=pltpu.VMEM((members, 3, 1, LANES), f32),
        in_specs=[WHOLE],
        out_specs=WHOLE,
        name="spread",
    )(near(field))
    states = exchanged(spread, "dev", DEV_FIRST)
    per_group = active // groups
    partial = pl.pallas_call(
        pairs_kernel,
        out_shape=pltpu.VMEM((members, 1, LANES), f32),
        in_specs=[WHOLE, WHOLE],
        out_specs=WHOLE,
        name="pairs",
    )(near(states), near(field))
    arrived = exchanged(partial, "dev", DEV_FIRST)
    slots = per_group // members
    out = jax.ShapeDtypeStruct((slots, 3), f32)
    scale = 1.0 / (count * groups * members)
    force, jerk = pl.pallas_call(
        lambda *refs: finish_kernel(scale, *refs),
        out_shape=(out, out),
        in_specs=[WHOLE],
        out_specs=(WHOLE, WHOLE),
        name="finish",
    )(near(arrived))
    return force.T, jerk.T


def solution(mesh):
    both = ("grp", "dev")
    return jax.shard_map(
        per_device,
        mesh=mesh,
        in_specs=(P(None, both), P(None, both), P(both), P()),
        out_specs=(P(None, both), P(None, both)),
        check_vma=False,
    )
```

```python
import jax
import jax.numpy as jnp
from jax import lax
from jax.experimental import pallas as pl
from jax.experimental.pallas import tpu as pltpu
from jax.sharding import PartitionSpec as P

SOFT = 0.0025
LANES = 128
YX = (4, 4)
ZC = (16, 2)
WHOLE = pl.BlockSpec(memory_space=pltpu.VMEM)
SCALARS = pl.BlockSpec(memory_space=pltpu.SMEM)


def turned(index, dims):
    major, minor = dims
    first = (index // minor + major // 2) % major
    second = (index % minor + (minor // 2 if minor > 2 else 0)) % minor
    return second * major + first


def exchanged(x, axis, dims):
    order = sorted(range(dims[0] * dims[1]), key=lambda index: turned(index, dims))
    return lax.all_to_all(x, axis, 0, 0, axis_index_groups=[order], tiled=True)


def pack_kernel(index_ref, pos_ref, vel_ref, mass_ref, out_ref):
    active = index_ref.shape[0]
    count = pos_ref.shape[1]
    groups = out_ref.shape[0]
    per_group = active // groups
    owner = lax.axis_index("grp") * lax.axis_size("dev") + lax.axis_index("dev")
    offset = owner * count
    mass = mass_ref[...]
    rows = jnp.concatenate([pos_ref[...], vel_ref[...], mass, jnp.zeros_like(mass)], axis=0)
    for g in range(groups):
        out_ref[g] = rows
    first = jnp.int32(0)
    step = active // 2
    while step:
        first = first + jnp.where(index_ref[first + (step - 1)] < offset, step, 0)
        step //= 2
    first = first + jnp.where(index_ref[first] < offset, 1, 0)
    lane = lax.broadcasted_iota(jnp.int32, (3, LANES), 1)
    for k in range(4):
        rank = jnp.minimum(first + k, active - 1)
        local = index_ref[rank] - offset

        @pl.when((first + k < active) & (local < count))
        def _():
            chunk = pl.ds(pl.multiple_of(local // LANES * LANES, LANES), LANES)
            here = lane == local % LANES
            pos = jnp.sum(jnp.where(here, pos_ref[:, chunk], 0.0), axis=1, keepdims=True)
            vel = jnp.sum(jnp.where(here, vel_ref[:, chunk], 0.0), axis=1, keepdims=True)
            row = turned(rank // per_group, YX)
            slot = rank % per_group
            slot = slot % 2 * (per_group // 2) + turned(slot // 2, ZC)
            state = jnp.where(lane == slot, pos, jnp.where(lane == slot + LANES // 2, vel, 0.0))
            for c in range(3):
                tile = pl.ds(c * LANES, LANES)
                out_ref[row, 7:8, tile] = out_ref[row, 7:8, tile] + state[c : c + 1]


def spread_kernel(in_ref, out_ref):
    for c in range(3):
        tile = pl.ds(c * LANES, LANES)
        total = in_ref[0, 7:8, tile]
        for g in range(1, in_ref.shape[0]):
            total = total + in_ref[g, 7:8, tile]
        for d in range(out_ref.shape[0]):
            out_ref[d, c] = total


def pairs_kernel(state_ref, field_ref, out_ref):
    sources, _, count = field_ref.shape
    width = 4
    rows = []
    for c in range(3):
        total = state_ref[0, c]
        for d in range(1, state_ref.shape[0]):
            total = total + state_ref[d, c]
        rows.append(total)
    packed = jnp.concatenate(rows + [jnp.zeros((5, LANES), jnp.float32)], axis=0).T
    lane = lax.broadcasted_iota(jnp.int32, (8, LANES), 1)
    half = LANES // 2
    zero = jnp.zeros((8, LANES), jnp.float32)
    results = []
    for top in range(0, half // 8, width):
        states = [
            [
                jnp.broadcast_to(packed[h + 8 * (top + i) : h + 8 * (top + i) + 8, c : c + 1], (8, LANES))
                for h in (0, half)
                for c in range(3)
            ]
            for i in range(width)
        ]

        def one_source(b, sums, states=states):
            sums = [list(s) for s in sums]
            for t in range(0, count, LANES):
                star = [jnp.broadcast_to(field_ref[b, c : c + 1, t : t + LANES], (8, LANES)) for c in range(7)]
                for act, s in zip(states, sums):
                    dx = [star[c] - act[c] for c in range(3)]
                    dv = [star[3 + c] - act[3 + c] for c in range(3)]
                    r2 = dx[0] * dx[0] + dx[1] * dx[1] + dx[2] * dx[2] + SOFT
                    inv = lax.rsqrt(r2)
                    rv = dx[0] * dv[0] + dx[1] * dv[1] + dx[2] * dv[2]
                    inv2 = inv * inv
                    weight = star[6] * inv * inv2
                    ratio = rv * inv2
                    for c in range(3):
                        pull = weight * dx[c]
                        s[c] = s[c] + pull
                        s[3 + c] = s[3 + c] + weight * dv[c]
                        s[6 + c] = s[6 + c] + ratio * pull
            return tuple(tuple(s) for s in sums)

        sums = lax.fori_loop(0, sources, one_source, ((zero,) * 9,) * width, unroll=2)
        first = 6 * (2 * top // (half // 8))
        for s in sums:
            result = zero
            for c in range(3):
                force = jnp.sum(s[c], axis=1, keepdims=True)
                jerk = jnp.sum(s[3 + c] - 3.0 * s[6 + c], axis=1, keepdims=True)
                result = jnp.where(lane == first + c, force, jnp.where(lane == first + 3 + c, jerk, result))
            results.append(result)
    for i in range(len(results) // 2):
        out_ref[pl.ds(8 * i, 8), 0, :] = results[i] + results[i + len(results) // 2]


def finish_kernel(scale, in_ref, force_ref, jerk_ref):
    total = in_ref[0]
    for d in range(1, in_ref.shape[0]):
        total = total + in_ref[d]
    total = total * scale
    for slot in range(force_ref.shape[0]):
        force_ref[slot : slot + 1, :] = total[:, 6 * slot : 6 * slot + 3]
        jerk_ref[slot : slot + 1, :] = total[:, 6 * slot + 3 : 6 * slot + 6]


def near(x):
    return pltpu.with_memory_space_constraint(x, pltpu.VMEM)


def per_device(positions, velocities, masses, active_index):
    groups, members = lax.axis_size("grp"), lax.axis_size("dev")
    count = positions.shape[1]
    active = active_index.shape[0]
    f32 = jnp.float32
    packed = pl.pallas_call(
        pack_kernel,
        out_shape=pltpu.VMEM((groups, 8, count), f32),
        in_specs=[SCALARS, WHOLE, WHOLE, WHOLE],
        out_specs=WHOLE,
        name="pack",
    )(active_index, positions, velocities, masses.reshape(1, count))
    field = exchanged(packed, "grp", YX)
    spread = pl.pallas_call(
        spread_kernel,
        out_shape=pltpu.VMEM((members, 3, 1, LANES), f32),
        in_specs=[WHOLE],
        out_specs=WHOLE,
        name="spread",
    )(near(field))
    states = exchanged(spread, "dev", ZC)
    per_group = active // groups
    partial = pl.pallas_call(
        pairs_kernel,
        out_shape=pltpu.VMEM((members, 1, LANES), f32),
        in_specs=[WHOLE, WHOLE],
        out_specs=WHOLE,
        name="pairs",
    )(near(states), near(field))
    arrived = exchanged(partial, "dev", ZC)
    slots = per_group // members
    out = jax.ShapeDtypeStruct((slots, 3), f32)
    scale = 1.0 / (count * groups * members)
    force, jerk = pl.pallas_call(
        lambda *refs: finish_kernel(scale, *refs),
        out_shape=(out, out),
        in_specs=[WHOLE],
        out_specs=(WHOLE, WHOLE),
        name="finish",
    )(near(arrived))
    return force.T, jerk.T


def solution(mesh):
    both = ("grp", "dev")
    return jax.shard_map(
        per_device,
        mesh=mesh,
        in_specs=(P(None, both), P(None, both), P(both), P()),
        out_specs=(P(None, both), P(None, both)),
        check_vma=False,
    )
```

```python
import jax
import jax.numpy as jnp
from jax import lax
from jax.experimental import pallas as pl
from jax.experimental.pallas import tpu as pltpu
from jax.sharding import PartitionSpec as P

SOFT = 0.0025
LANES = 128
YX = (4, 4)
ZC = (16, 2)
WHOLE = pl.BlockSpec(memory_space=pltpu.VMEM)
SCALARS = pl.BlockSpec(memory_space=pltpu.SMEM)


def turned(index, dims):
    major, minor = dims
    first = (index // minor + major // 2) % major
    second = (index % minor + (minor // 2 if minor > 2 else 0)) % minor
    return second * major + first


def exchanged(x, axis, dims):
    order = sorted(range(dims[0] * dims[1]), key=lambda index: turned(index, dims))
    return lax.all_to_all(x, axis, 0, 0, axis_index_groups=[order], tiled=True)


def pack_kernel(index_ref, pos_ref, vel_ref, mass_ref, out_ref):
    active = index_ref.shape[0]
    count = pos_ref.shape[1]
    groups = out_ref.shape[0]
    per_group = active // groups
    owner = lax.axis_index("grp") * lax.axis_size("dev") + lax.axis_index("dev")
    offset = owner * count
    mass = mass_ref[...]
    rows = jnp.concatenate([pos_ref[...], vel_ref[...], mass, jnp.zeros_like(mass)], axis=0)
    for g in range(groups):
        out_ref[g] = rows
    first = jnp.int32(0)
    step = active // 2
    while step:
        first = first + jnp.where(index_ref[first + (step - 1)] < offset, step, 0)
        step //= 2
    first = first + jnp.where(index_ref[first] < offset, 1, 0)
    lane = lax.broadcasted_iota(jnp.int32, (3, LANES), 1)
    for k in range(4):
        rank = jnp.minimum(first + k, active - 1)
        local = index_ref[rank] - offset

        @pl.when((first + k < active) & (local < count))
        def _():
            chunk = pl.ds(pl.multiple_of(local // LANES * LANES, LANES), LANES)
            here = lane == local % LANES
            pos = jnp.sum(jnp.where(here, pos_ref[:, chunk], 0.0), axis=1, keepdims=True)
            vel = jnp.sum(jnp.where(here, vel_ref[:, chunk], 0.0), axis=1, keepdims=True)
            row = turned(rank // per_group, YX)
            slot = rank % per_group
            slot = slot % 2 * (per_group // 2) + turned(slot // 2, ZC)
            state = jnp.where(lane == slot, pos, jnp.where(lane == slot + LANES // 2, vel, 0.0))
            for c in range(3):
                tile = pl.ds(c * LANES, LANES)
                out_ref[row, 7:8, tile] = out_ref[row, 7:8, tile] + state[c : c + 1]


def spread_kernel(in_ref, out_ref):
    for c in range(3):
        tile = pl.ds(c * LANES, LANES)
        total = in_ref[0, 7:8, tile]
        for g in range(1, in_ref.shape[0]):
            total = total + in_ref[g, 7:8, tile]
        for d in range(out_ref.shape[0]):
            out_ref[d, c] = total


def in_parts(x, count):
    parts = []
    for _ in range(count):
        parts.append(x.astype(jnp.bfloat16).astype(jnp.float32))
        x = x - parts[-1]
    return parts


def pairs_kernel(state_ref, field_ref, out_ref):
    sources, _, count = field_ref.shape
    half = LANES // 2
    f32, bf16 = jnp.float32, jnp.bfloat16
    rows = []
    for c in range(3):
        total = state_ref[0, c]
        for d in range(1, state_ref.shape[0]):
            total = total + state_ref[d, c]
        rows.append(total)
    state = jnp.concatenate(rows + [jnp.zeros((5, LANES), f32)], axis=0)
    packed = state.T
    actives = [
        [jnp.broadcast_to(packed[h + g : h + g + 8, c : c + 1], (8, LANES)) for h in (0, half) for c in range(3)]
        for g in range(0, half, 8)
    ]
    pos0, vel0 = state[0:3, 0:1], state[0:3, half : half + 1]
    origin = jnp.concatenate([pos0, vel0, jnp.zeros((2, 1), f32)], axis=0)
    row = lax.broadcasted_iota(jnp.int32, (8, count), 0)
    step = 2 * LANES

    def one_source(b, sums):
        stars = jnp.where(row == 6, 1.0, field_ref[b] - origin)
        high, middle, low = in_parts(stars, 3)
        stars = jnp.concatenate(
            [
                jnp.concatenate([high, middle], axis=0).astype(bf16),
                jnp.concatenate([low, jnp.zeros_like(low)], axis=0).astype(bf16),
            ],
            axis=0,
        )
        for start in range(0, count, step):
            weights, ratios = [], []
            for t in range(start, start + step, LANES):
                star = [jnp.broadcast_to(field_ref[b, c : c + 1, t : t + LANES], (8, LANES)) for c in range(7)]
                column_w, column_r = [], []
                for act in actives:
                    dx = [star[c] - act[c] for c in range(3)]
                    dv = [star[3 + c] - act[3 + c] for c in range(3)]
                    r2 = dx[0] * dx[0] + dx[1] * dx[1] + dx[2] * dx[2] + SOFT
                    inv = lax.rsqrt(r2)
                    rv = dx[0] * dv[0] + dx[1] * dv[1] + dx[2] * dv[2]
                    inv2 = inv * inv
                    weight = star[6] * inv * inv2
                    column_w.append(weight)
                    column_r.append(rv * inv2 * weight)
                weights.append(jnp.concatenate(column_w, axis=0))
                ratios.append(jnp.concatenate(column_r, axis=0))
            parts = in_parts(jnp.concatenate(weights, axis=1), 2) + in_parts(jnp.concatenate(ratios, axis=1), 2)
            sums = sums + lax.dot_general(
                stars[:, start : start + step],
                jnp.concatenate([p.astype(bf16) for p in parts], axis=0),
                (((1,), (1,)), ((), ())),
                preferred_element_type=f32,
            )
        return sums

    sums = jnp.zeros((32, 4 * half), f32)
    for b in range(sources):
        sums = one_source(b, sums)
    sums = sums[0:8] + sums[8:16] + sums[16:24]
    by_weight, by_ratio = sums[:, :LANES], sums[:, LANES:]
    by_weight = by_weight + pltpu.roll(by_weight, half, 1)
    by_ratio = by_ratio + pltpu.roll(by_ratio, half, 1)
    pos = state[0:3] - pos0
    vel = pltpu.roll(state, half, 1)[0:3] - vel0
    force = by_weight[0:3] - pos * by_weight[6:7]
    jerk = by_weight[3:6] - vel * by_weight[6:7] - 3.0 * (by_ratio[0:3] - pos * by_ratio[6:7])
    even = jnp.concatenate([force, jerk, jnp.zeros((2, LANES), f32)], axis=0)
    odd = pltpu.roll(even, LANES - half // 2, 1)
    out = jnp.concatenate([even[0:6], odd[0:6], jnp.zeros((LANES - 12, LANES), f32)], axis=0).T
    for i in range(0, half // 2, 8):
        out_ref[pl.ds(i, 8), 0, :] = out[i : i + 8]


def finish_kernel(scale, in_ref, force_ref, jerk_ref):
    total = in_ref[0]
    for d in range(1, in_ref.shape[0]):
        total = total + in_ref[d]
    total = total * scale
    for slot in range(force_ref.shape[0]):
        force_ref[slot : slot + 1, :] = total[:, 6 * slot : 6 * slot + 3]
        jerk_ref[slot : slot + 1, :] = total[:, 6 * slot + 3 : 6 * slot + 6]


def near(x):
    return pltpu.with_memory_space_constraint(x, pltpu.VMEM)


def per_device(positions, velocities, masses, active_index):
    groups, members = lax.axis_size("grp"), lax.axis_size("dev")
    count = positions.shape[1]
    active = active_index.shape[0]
    f32 = jnp.float32
    packed = pl.pallas_call(
        pack_kernel,
        out_shape=pltpu.VMEM((groups, 8, count), f32),
        in_specs=[SCALARS, WHOLE, WHOLE, WHOLE],
        out_specs=WHOLE,
        name="pack",
    )(active_index, positions, velocities, masses.reshape(1, count))
    field = exchanged(packed, "grp", YX)
    spread = pl.pallas_call(
        spread_kernel,
        out_shape=pltpu.VMEM((members, 3, 1, LANES), f32),
        in_specs=[WHOLE],
        out_specs=WHOLE,
        name="spread",
    )(near(field))
    states = exchanged(spread, "dev", ZC)
    per_group = active // groups
    partial = pl.pallas_call(
        pairs_kernel,
        out_shape=pltpu.VMEM((members, 1, LANES), f32),
        in_specs=[WHOLE, WHOLE],
        out_specs=WHOLE,
        name="pairs",
    )(near(states), near(field))
    arrived = exchanged(partial, "dev", ZC)
    slots = per_group // members
    out = jax.ShapeDtypeStruct((slots, 3), f32)
    scale = 1.0 / (count * groups * members)
    force, jerk = pl.pallas_call(
        lambda *refs: finish_kernel(scale, *refs),
        out_shape=(out, out),
        in_specs=[WHOLE],
        out_specs=(WHOLE, WHOLE),
        name="finish",
    )(near(arrived))
    return force.T, jerk.T


def solution(mesh):
    both = ("grp", "dev")
    return jax.shard_map(
        per_device,
        mesh=mesh,
        in_specs=(P(None, both), P(None, both), P(both), P()),
        out_specs=(P(None, both), P(None, both)),
        check_vma=False,
    )
```

```python
import jax
import jax.numpy as jnp
from jax import lax
from jax.experimental import pallas as pl
from jax.experimental.pallas import tpu as pltpu
from jax.sharding import PartitionSpec as P

SOFT = 0.0025
LANES = 128
GRP_HEAD = (10, 0)
DEV_HEAD = (17, 1, 0)
GRP_ORDER = GRP_HEAD + tuple(
    g for g in ((2 + i) % 4 * 4 + (2 + j) % 4 for j in range(4) for i in range(4)) if g not in GRP_HEAD
)
DEV_ORDER = DEV_HEAD + tuple(
    d for d in ((8 + i) % 16 * 2 + c for c in (1, 0) for i in range(16)) if d not in DEV_HEAD
)
WHOLE = pl.BlockSpec(memory_space=pltpu.VMEM)
SCALARS = pl.BlockSpec(memory_space=pltpu.SMEM)


def place_in(order, index):
    places = [order.index(i) for i in range(len(order))]
    words = [sum(p << 8 * n for n, p in enumerate(places[i : i + 4])) for i in range(0, len(places), 4)]
    word = jnp.int32(words[0])
    for i in range(1, len(words)):
        word = jnp.where(index >= 4 * i, words[i], word)
    return (word >> 8 * (index & 3)) & 255


def exchanged(x, axis, order):
    return lax.all_to_all(x, axis, 0, 0, axis_index_groups=[list(order)], tiled=True)


def pack_kernel(index_ref, pos_ref, vel_ref, mass_ref, out_ref):
    active = index_ref.shape[0]
    count = pos_ref.shape[1]
    groups = out_ref.shape[0]
    per_group = active // groups
    owner = lax.axis_index("grp") * lax.axis_size("dev") + lax.axis_index("dev")
    offset = owner * count
    mass = mass_ref[...]
    rows = jnp.concatenate([pos_ref[...], vel_ref[...], mass, jnp.zeros_like(mass)], axis=0)
    for g in range(groups):
        out_ref[g] = rows
    first = jnp.int32(0)
    step = active // 2
    while step:
        first = first + jnp.where(index_ref[first + (step - 1)] < offset, step, 0)
        step //= 2
    first = first + jnp.where(index_ref[first] < offset, 1, 0)
    lane = lax.broadcasted_iota(jnp.int32, (3, LANES), 1)
    rows = []
    for k in range(4):
        rank = jnp.minimum(first + k, active - 1)
        local = index_ref[rank] - offset
        held = (first + k < active) & (local < count)
        local = jnp.clip(local, 0, count - 1)
        chunk = pl.ds(pl.multiple_of(lax.div(local, LANES) * LANES, LANES), LANES)
        here = lane == lax.rem(local, LANES)
        pos = jnp.sum(jnp.where(here, pos_ref[:, chunk], 0.0), axis=1, keepdims=True)
        vel = jnp.sum(jnp.where(here, vel_ref[:, chunk], 0.0), axis=1, keepdims=True)
        slot = lax.rem(rank, per_group)
        slot = (slot & 1) * (per_group // 2) + place_in(DEV_ORDER, slot >> 1)
        slot = jnp.where(held, slot, LANES)
        state = jnp.where(lane == slot, pos, jnp.where(lane == slot + LANES // 2, vel, 0.0))
        rows.append((place_in(GRP_ORDER, lax.div(rank, per_group)), state))
    for row, state in rows:
        for c in range(3):
            tile = pl.ds(c * LANES, LANES)
            out_ref[row, 7:8, tile] = out_ref[row, 7:8, tile] + state[c : c + 1]


def spread_kernel(in_ref, out_ref):
    for c in range(3):
        tile = pl.ds(c * LANES, LANES)
        total = in_ref[0, 7:8, tile]
        for g in range(1, in_ref.shape[0]):
            total = total + in_ref[g, 7:8, tile]
        for d in range(out_ref.shape[0]):
            out_ref[d, c] = total


def in_parts(x, count):
    parts = []
    for _ in range(count):
        parts.append(x.astype(jnp.bfloat16).astype(jnp.float32))
        x = x - parts[-1]
    return parts


def pairs_kernel(state_ref, field_ref, out_ref):
    sources, _, count = field_ref.shape
    half = LANES // 2
    f32, bf16 = jnp.float32, jnp.bfloat16
    rows = []
    for c in range(3):
        total = state_ref[0, c]
        for d in range(1, state_ref.shape[0]):
            total = total + state_ref[d, c]
        rows.append(total)
    state = jnp.concatenate(rows + [jnp.zeros((5, LANES), f32)], axis=0)
    packed = state.T
    actives = [
        [jnp.broadcast_to(packed[h + g : h + g + 8, c : c + 1], (8, LANES)) for h in (0, half) for c in range(3)]
        for g in range(0, half, 8)
    ]
    pos0, vel0 = state[0:3, 0:1], state[0:3, half : half + 1]
    origin = jnp.concatenate([pos0, vel0, jnp.zeros((2, 1), f32)], axis=0)
    row = lax.broadcasted_iota(jnp.int32, (8, count), 0)
    step = 2 * LANES

    def one_source(b, sums):
        stars = jnp.where(row == 6, 1.0, field_ref[b] - origin)
        high, middle, low = in_parts(stars, 3)
        stars = jnp.concatenate(
            [
                jnp.concatenate([high, middle], axis=0).astype(bf16),
                jnp.concatenate([low, jnp.zeros_like(low)], axis=0).astype(bf16),
            ],
            axis=0,
        )
        for start in range(0, count, step):
            weights, ratios = [], []
            for t in range(start, start + step, LANES):
                star = [jnp.broadcast_to(field_ref[b, c : c + 1, t : t + LANES], (8, LANES)) for c in range(7)]
                column_w, column_r = [], []
                for act in actives:
                    dx = [star[c] - act[c] for c in range(3)]
                    dv = [star[3 + c] - act[3 + c] for c in range(3)]
                    r2 = dx[0] * dx[0] + dx[1] * dx[1] + dx[2] * dx[2] + SOFT
                    inv = lax.rsqrt(r2)
                    rv = dx[0] * dv[0] + dx[1] * dv[1] + dx[2] * dv[2]
                    inv2 = inv * inv
                    weight = star[6] * inv * inv2
                    column_w.append(weight)
                    column_r.append(rv * inv2 * weight)
                weights.append(jnp.concatenate(column_w, axis=0))
                ratios.append(jnp.concatenate(column_r, axis=0))
            parts = in_parts(jnp.concatenate(weights, axis=1), 2) + in_parts(jnp.concatenate(ratios, axis=1), 2)
            sums = sums + lax.dot_general(
                stars[:, start : start + step],
                jnp.concatenate([p.astype(bf16) for p in parts], axis=0),
                (((1,), (1,)), ((), ())),
                preferred_element_type=f32,
            )
        return sums

    sums = jnp.zeros((32, 4 * half), f32)
    for b in range(sources):
        sums = one_source(b, sums)
    sums = sums[0:8] + sums[8:16] + sums[16:24]
    by_weight, by_ratio = sums[:, :LANES], sums[:, LANES:]
    by_weight = by_weight + pltpu.roll(by_weight, half, 1)
    by_ratio = by_ratio + pltpu.roll(by_ratio, half, 1)
    pos = state[0:3] - pos0
    vel = pltpu.roll(state, half, 1)[0:3] - vel0
    force = by_weight[0:3] - pos * by_weight[6:7]
    jerk = by_weight[3:6] - vel * by_weight[6:7] - 3.0 * (by_ratio[0:3] - pos * by_ratio[6:7])
    even = jnp.concatenate([force, jerk, jnp.zeros((2, LANES), f32)], axis=0)
    odd = pltpu.roll(even, LANES - half // 2, 1)
    out = jnp.concatenate([even[0:6], odd[0:6], jnp.zeros((LANES - 12, LANES), f32)], axis=0).T
    for i in range(0, half // 2, 8):
        out_ref[pl.ds(i, 8), 0, :] = out[i : i + 8]


def finish_kernel(scale, in_ref, force_ref, jerk_ref):
    total = in_ref[0]
    for d in range(1, in_ref.shape[0]):
        total = total + in_ref[d]
    total = total * scale
    for slot in range(force_ref.shape[0]):
        force_ref[slot : slot + 1, :] = total[:, 6 * slot : 6 * slot + 3]
        jerk_ref[slot : slot + 1, :] = total[:, 6 * slot + 3 : 6 * slot + 6]


def near(x):
    return pltpu.with_memory_space_constraint(x, pltpu.VMEM)


def per_device(positions, velocities, masses, active_index):
    groups, members = lax.axis_size("grp"), lax.axis_size("dev")
    count = positions.shape[1]
    active = active_index.shape[0]
    f32 = jnp.float32
    packed = pl.pallas_call(
        pack_kernel,
        out_shape=pltpu.VMEM((groups, 8, count), f32),
        in_specs=[SCALARS, WHOLE, WHOLE, WHOLE],
        out_specs=WHOLE,
        name="pack",
    )(active_index, positions, velocities, masses.reshape(1, count))
    field = exchanged(packed, "grp", GRP_ORDER)
    spread = pl.pallas_call(
        spread_kernel,
        out_shape=pltpu.VMEM((members, 3, 1, LANES), f32),
        in_specs=[WHOLE],
        out_specs=WHOLE,
        name="spread",
    )(near(field))
    states = exchanged(spread, "dev", DEV_ORDER)
    per_group = active // groups
    partial = pl.pallas_call(
        pairs_kernel,
        out_shape=pltpu.VMEM((members, 1, LANES), f32),
        in_specs=[WHOLE, WHOLE],
        out_specs=WHOLE,
        name="pairs",
    )(near(states), near(field))
    arrived = exchanged(partial, "dev", DEV_ORDER)
    slots = per_group // members
    out = jax.ShapeDtypeStruct((slots, 3), f32)
    scale = 1.0 / (count * groups * members)
    force, jerk = pl.pallas_call(
        lambda *refs: finish_kernel(scale, *refs),
        out_shape=(out, out),
        in_specs=[WHOLE],
        out_specs=(WHOLE, WHOLE),
        name="finish",
    )(near(arrived))
    return force.T, jerk.T


def solution(mesh):
    both = ("grp", "dev")
    return jax.shard_map(
        per_device,
        mesh=mesh,
        in_specs=(P(None, both), P(None, both), P(both), P()),
        out_specs=(P(None, both), P(None, both)),
        check_vma=False,
    )
```

```python
import jax
import jax.numpy as jnp
from jax import lax
from jax.experimental import pallas as pl
from jax.experimental.pallas import tpu as pltpu
from jax.sharding import PartitionSpec as P

SOFT = 0.0025
LANES = 128
GRP_HEAD = (10, 0, 8, 2, 12, 3)
DEV_HEAD = (17,)
GRP_ORDER = GRP_HEAD + tuple(
    g for g in ((2 + i) % 4 * 4 + (2 + j) % 4 for j in range(4) for i in range(4)) if g not in GRP_HEAD
)
DEV_ORDER = DEV_HEAD + tuple(
    d for d in (2 * z + c for z in sorted(range(16), key=lambda z: min(z, 16 - z)) for c in (1, 0)) if d not in DEV_HEAD
)
WHOLE = pl.BlockSpec(memory_space=pltpu.VMEM)
SCALARS = pl.BlockSpec(memory_space=pltpu.SMEM)


def place_in(order, index):
    places = [order.index(i) for i in range(len(order))]
    words = [sum(p << 8 * n for n, p in enumerate(places[i : i + 4])) for i in range(0, len(places), 4)]
    word = jnp.int32(words[0])
    for i in range(1, len(words)):
        word = jnp.where(index >= 4 * i, words[i], word)
    return (word >> 8 * (index & 3)) & 255


def exchanged(x, axis, order):
    return lax.all_to_all(x, axis, 0, 0, axis_index_groups=[list(order)], tiled=True)


def pack_kernel(index_ref, pos_ref, vel_ref, mass_ref, out_ref):
    active = index_ref.shape[0]
    count = pos_ref.shape[1]
    groups = out_ref.shape[0]
    per_group = active // groups
    owner = lax.axis_index("grp") * lax.axis_size("dev") + lax.axis_index("dev")
    offset = owner * count
    mass = mass_ref[...]
    rows = jnp.concatenate([pos_ref[...], vel_ref[...], mass, jnp.zeros_like(mass)], axis=0)
    for g in range(groups):
        out_ref[g] = rows
    first = jnp.int32(0)
    step = active // 2
    while step:
        first = first + jnp.where(index_ref[first + (step - 1)] < offset, step, 0)
        step //= 2
    first = first + jnp.where(index_ref[first] < offset, 1, 0)
    lane = lax.broadcasted_iota(jnp.int32, (3, LANES), 1)
    rows = []
    for k in range(4):
        rank = jnp.minimum(first + k, active - 1)
        local = index_ref[rank] - offset
        held = (first + k < active) & (local < count)
        local = jnp.clip(local, 0, count - 1)
        chunk = pl.ds(pl.multiple_of(lax.div(local, LANES) * LANES, LANES), LANES)
        here = lane == lax.rem(local, LANES)
        pos = jnp.sum(jnp.where(here, pos_ref[:, chunk], 0.0), axis=1, keepdims=True)
        vel = jnp.sum(jnp.where(here, vel_ref[:, chunk], 0.0), axis=1, keepdims=True)
        slot = lax.rem(rank, per_group)
        slot = (slot & 1) * (per_group // 2) + place_in(DEV_ORDER, slot >> 1)
        slot = jnp.where(held, slot, LANES)
        state = jnp.where(lane == slot, pos, jnp.where(lane == slot + LANES // 2, vel, 0.0))
        rows.append((place_in(GRP_ORDER, lax.div(rank, per_group)), state))
    for row, state in rows:
        for c in range(3):
            tile = pl.ds(c * LANES, LANES)
            out_ref[row, 7:8, tile] = out_ref[row, 7:8, tile] + state[c : c + 1]


def spread_kernel(in_ref, out_ref):
    for c in range(3):
        tile = pl.ds(c * LANES, LANES)
        total = in_ref[0, 7:8, tile]
        for g in range(1, in_ref.shape[0]):
            total = total + in_ref[g, 7:8, tile]
        for d in range(out_ref.shape[0]):
            out_ref[d, c] = total


def in_parts(x, count):
    parts = []
    for _ in range(count):
        parts.append(x.astype(jnp.bfloat16).astype(jnp.float32))
        x = x - parts[-1]
    return parts


def pairs_kernel(state_ref, field_ref, out_ref):
    sources, _, count = field_ref.shape
    half = LANES // 2
    f32, bf16 = jnp.float32, jnp.bfloat16
    rows = []
    for c in range(3):
        total = state_ref[0, c]
        for d in range(1, state_ref.shape[0]):
            total = total + state_ref[d, c]
        rows.append(total)
    state = jnp.concatenate(rows + [jnp.zeros((5, LANES), f32)], axis=0)
    packed = state.T
    actives = [
        [jnp.broadcast_to(packed[h + g : h + g + 8, c : c + 1], (8, LANES)) for h in (0, half) for c in range(3)]
        for g in range(0, half, 8)
    ]
    pos0, vel0 = state[0:3, 0:1], state[0:3, half : half + 1]
    origin = jnp.concatenate([pos0, vel0, jnp.zeros((2, 1), f32)], axis=0)
    row = lax.broadcasted_iota(jnp.int32, (8, count), 0)
    step = 2 * LANES

    def one_source(b, sums):
        stars = jnp.where(row == 6, 1.0, field_ref[b] - origin)
        high, middle, low = in_parts(stars, 3)
        stars = jnp.concatenate(
            [
                jnp.concatenate([high, middle], axis=0).astype(bf16),
                jnp.concatenate([low, jnp.zeros_like(low)], axis=0).astype(bf16),
            ],
            axis=0,
        )
        for start in range(0, count, step):
            weights, ratios = [], []
            for t in range(start, start + step, LANES):
                star = [jnp.broadcast_to(field_ref[b, c : c + 1, t : t + LANES], (8, LANES)) for c in range(7)]
                column_w, column_r = [], []
                for act in actives:
                    dx = [star[c] - act[c] for c in range(3)]
                    dv = [star[3 + c] - act[3 + c] for c in range(3)]
                    r2 = dx[0] * dx[0] + dx[1] * dx[1] + dx[2] * dx[2] + SOFT
                    inv = lax.rsqrt(r2)
                    rv = dx[0] * dv[0] + dx[1] * dv[1] + dx[2] * dv[2]
                    inv2 = inv * inv
                    weight = star[6] * inv * inv2
                    column_w.append(weight)
                    column_r.append(rv * inv2 * weight)
                weights.append(jnp.concatenate(column_w, axis=0))
                ratios.append(jnp.concatenate(column_r, axis=0))
            parts = in_parts(jnp.concatenate(weights, axis=1), 2) + in_parts(jnp.concatenate(ratios, axis=1), 2)
            sums = sums + lax.dot_general(
                stars[:, start : start + step],
                jnp.concatenate([p.astype(bf16) for p in parts], axis=0),
                (((1,), (1,)), ((), ())),
                preferred_element_type=f32,
            )
        return sums

    sums = jnp.zeros((32, 4 * half), f32)
    for b in range(sources):
        sums = one_source(b, sums)
    sums = sums[0:8] + sums[8:16] + sums[16:24]
    by_weight, by_ratio = sums[:, :LANES], sums[:, LANES:]
    by_weight = by_weight + pltpu.roll(by_weight, half, 1)
    by_ratio = by_ratio + pltpu.roll(by_ratio, half, 1)
    pos = state[0:3] - pos0
    vel = pltpu.roll(state, half, 1)[0:3] - vel0
    force = by_weight[0:3] - pos * by_weight[6:7]
    jerk = by_weight[3:6] - vel * by_weight[6:7] - 3.0 * (by_ratio[0:3] - pos * by_ratio[6:7])
    even = jnp.concatenate([force, jerk, jnp.zeros((2, LANES), f32)], axis=0)
    odd = pltpu.roll(even, LANES - half // 2, 1)
    out = jnp.concatenate([even[0:6], odd[0:6], jnp.zeros((LANES - 12, LANES), f32)], axis=0).T
    for i in range(0, half // 2, 8):
        out_ref[pl.ds(i, 8), 0, :] = out[i : i + 8]


def finish_kernel(scale, in_ref, force_ref, jerk_ref):
    total = in_ref[0]
    for d in range(1, in_ref.shape[0]):
        total = total + in_ref[d]
    total = total * scale
    for slot in range(force_ref.shape[0]):
        force_ref[slot : slot + 1, :] = total[:, 6 * slot : 6 * slot + 3]
        jerk_ref[slot : slot + 1, :] = total[:, 6 * slot + 3 : 6 * slot + 6]


def near(x):
    return pltpu.with_memory_space_constraint(x, pltpu.VMEM)


def per_device(positions, velocities, masses, active_index):
    groups, members = lax.axis_size("grp"), lax.axis_size("dev")
    count = positions.shape[1]
    active = active_index.shape[0]
    f32 = jnp.float32
    packed = pl.pallas_call(
        pack_kernel,
        out_shape=pltpu.VMEM((groups, 8, count), f32),
        in_specs=[SCALARS, WHOLE, WHOLE, WHOLE],
        out_specs=WHOLE,
        name="pack",
    )(active_index, positions, velocities, masses.reshape(1, count))
    field = exchanged(packed, "grp", GRP_ORDER)
    spread = pl.pallas_call(
        spread_kernel,
        out_shape=pltpu.VMEM((members, 3, 1, LANES), f32),
        in_specs=[WHOLE],
        out_specs=WHOLE,
        name="spread",
    )(near(field))
    states = exchanged(spread, "dev", DEV_ORDER)
    per_group = active // groups
    partial = pl.pallas_call(
        pairs_kernel,
        out_shape=pltpu.VMEM((members, 1, LANES), f32),
        in_specs=[WHOLE, WHOLE],
        out_specs=WHOLE,
        name="pairs",
    )(near(states), near(field))
    arrived = exchanged(partial, "dev", DEV_ORDER)
    slots = per_group // members
    out = jax.ShapeDtypeStruct((slots, 3), f32)
    scale = 1.0 / (count * groups * members)
    force, jerk = pl.pallas_call(
        lambda *refs: finish_kernel(scale, *refs),
        out_shape=(out, out),
        in_specs=[WHOLE],
        out_specs=(WHOLE, WHOLE),
        name="finish",
    )(near(arrived))
    return force.T, jerk.T


def solution(mesh):
    both = ("grp", "dev")
    return jax.shard_map(
        per_device,
        mesh=mesh,
        in_specs=(P(None, both), P(None, both), P(both), P()),
        out_specs=(P(None, both), P(None, both)),
        check_vma=False,
    )
```

```python
import jax
import jax.numpy as jnp
from jax import lax
from jax.experimental import pallas as pl
from jax.experimental.pallas import tpu as pltpu
from jax.sharding import PartitionSpec as P

SOFT = 0.0025
LANES = 128
GRP_HEAD = (10, 0, 8, 2, 12, 3)
DEV_HEAD = (17,)
GRP_ORDER = GRP_HEAD + tuple(
    g for g in ((2 + i) % 4 * 4 + (2 + j) % 4 for j in range(4) for i in range(4)) if g not in GRP_HEAD
)
DEV_ORDER = DEV_HEAD + tuple(
    d for d in (2 * z + c for z in sorted(range(16), key=lambda z: min(z, 16 - z)) for c in (1, 0)) if d not in DEV_HEAD
)
WHOLE = pl.BlockSpec(memory_space=pltpu.VMEM)
SCALARS = pl.BlockSpec(memory_space=pltpu.SMEM)


def place_in(order, index):
    places = [order.index(i) for i in range(len(order))]
    words = [sum(p << 8 * n for n, p in enumerate(places[i : i + 4])) for i in range(0, len(places), 4)]
    word = jnp.int32(words[0])
    for i in range(1, len(words)):
        word = jnp.where(index >= 4 * i, words[i], word)
    return (word >> 8 * (index & 3)) & 255


def exchanged(x, axis, order):
    return lax.all_to_all(x, axis, 0, 0, axis_index_groups=[list(order)], tiled=True)


def pack_kernel(index_ref, pos_ref, vel_ref, mass_ref, out_ref):
    active = index_ref.shape[0]
    count = pos_ref.shape[1]
    groups = out_ref.shape[0]
    per_group = active // groups
    owner = lax.axis_index("grp") * lax.axis_size("dev") + lax.axis_index("dev")
    offset = owner * count
    mass = mass_ref[...]
    rows = jnp.concatenate([pos_ref[...], vel_ref[...], mass, jnp.zeros_like(mass)], axis=0)
    for g in range(groups):
        out_ref[g] = rows
    first = jnp.int32(0)
    step = active // 2
    while step:
        first = first + jnp.where(index_ref[first + (step - 1)] < offset, step, 0)
        step //= 2
    first = first + jnp.where(index_ref[first] < offset, 1, 0)
    lane = lax.broadcasted_iota(jnp.int32, (3, LANES), 1)
    rows = []
    for k in range(4):
        rank = jnp.minimum(first + k, active - 1)
        local = index_ref[rank] - offset
        held = (first + k < active) & (local < count)
        local = jnp.clip(local, 0, count - 1)
        chunk = pl.ds(pl.multiple_of(lax.div(local, LANES) * LANES, LANES), LANES)
        here = lane == lax.rem(local, LANES)
        pos = jnp.sum(jnp.where(here, pos_ref[:, chunk], 0.0), axis=1, keepdims=True)
        vel = jnp.sum(jnp.where(here, vel_ref[:, chunk], 0.0), axis=1, keepdims=True)
        slot = lax.rem(rank, per_group)
        slot = (slot & 1) * (per_group // 2) + place_in(DEV_ORDER, slot >> 1)
        slot = jnp.where(held, slot, LANES)
        state = jnp.where(lane == slot, pos, jnp.where(lane == slot + LANES // 2, vel, 0.0))
        rows.append((place_in(GRP_ORDER, lax.div(rank, per_group)), state))
    for row, state in rows:
        for c in range(3):
            tile = pl.ds(c * LANES, LANES)
            out_ref[row, 7:8, tile] = out_ref[row, 7:8, tile] + state[c : c + 1]


def spread_kernel(in_ref, out_ref):
    for c in range(3):
        tile = pl.ds(c * LANES, LANES)
        total = in_ref[0, 7:8, tile]
        for g in range(1, in_ref.shape[0]):
            total = total + in_ref[g, 7:8, tile]
        for d in range(out_ref.shape[0]):
            out_ref[d, c] = total


def in_parts(x, count):
    parts = []
    for _ in range(count):
        parts.append(x.astype(jnp.bfloat16).astype(jnp.float32))
        x = x - parts[-1]
    return parts


def pairs_kernel(state_ref, field_ref, out_ref):
    sources, _, count = field_ref.shape
    half = LANES // 2
    f32, bf16 = jnp.float32, jnp.bfloat16
    rows = []
    for c in range(3):
        total = state_ref[0, c]
        for d in range(1, state_ref.shape[0]):
            total = total + state_ref[d, c]
        rows.append(total)
    state = jnp.concatenate(rows + [jnp.zeros((5, LANES), f32)], axis=0)
    packed = state.T
    actives = [
        [jnp.broadcast_to(packed[h + g : h + g + 8, c : c + 1], (8, LANES)) for h in (0, half) for c in range(3)]
        for g in range(0, half, 8)
    ]
    pos0, vel0 = state[0:3, 0:1], state[0:3, half : half + 1]
    origin = jnp.concatenate([pos0, vel0, jnp.zeros((2, 1), f32)], axis=0)
    row = lax.broadcasted_iota(jnp.int32, (8, count), 0)
    step = 2 * LANES

    def one_source(b, sums):
        stars = field_ref[b] - origin
        stars = jnp.where(row == 6, stars, stars * field_ref[b, 6:7, :])
        high, middle, low = in_parts(stars, 3)
        stars = jnp.concatenate(
            [
                jnp.concatenate([high, middle], axis=0).astype(bf16),
                jnp.concatenate([low, jnp.zeros_like(low)], axis=0).astype(bf16),
            ],
            axis=0,
        )
        for start in range(0, count, step):
            weights, ratios = [], []
            for t in range(start, start + step, LANES):
                star = [jnp.broadcast_to(field_ref[b, c : c + 1, t : t + LANES], (8, LANES)) for c in range(6)]
                column_w, column_r = [], []
                for act in actives:
                    dx = [star[c] - act[c] for c in range(3)]
                    dv = [star[3 + c] - act[3 + c] for c in range(3)]
                    r2 = dx[0] * dx[0] + dx[1] * dx[1] + dx[2] * dx[2] + SOFT
                    inv = lax.rsqrt(r2)
                    rv = dx[0] * dv[0] + dx[1] * dv[1] + dx[2] * dv[2]
                    inv2 = inv * inv
                    weight = inv * inv2
                    column_w.append(weight)
                    column_r.append(rv * inv2 * weight)
                weights.append(jnp.concatenate(column_w, axis=0))
                ratios.append(jnp.concatenate(column_r, axis=0))
            parts = in_parts(jnp.concatenate(weights, axis=1), 2) + in_parts(jnp.concatenate(ratios, axis=1), 2)
            sums = sums + lax.dot_general(
                stars[:, start : start + step],
                jnp.concatenate([p.astype(bf16) for p in parts], axis=0),
                (((1,), (1,)), ((), ())),
                preferred_element_type=f32,
            )
        return sums

    sums = jnp.zeros((32, 4 * half), f32)
    for b in range(sources):
        sums = one_source(b, sums)
    sums = sums[0:8] + sums[8:16] + sums[16:24]
    by_weight, by_ratio = sums[:, :LANES], sums[:, LANES:]
    by_weight = by_weight + pltpu.roll(by_weight, half, 1)
    by_ratio = by_ratio + pltpu.roll(by_ratio, half, 1)
    pos = state[0:3] - pos0
    vel = pltpu.roll(state, half, 1)[0:3] - vel0
    force = by_weight[0:3] - pos * by_weight[6:7]
    jerk = by_weight[3:6] - vel * by_weight[6:7] - 3.0 * (by_ratio[0:3] - pos * by_ratio[6:7])
    even = jnp.concatenate([force, jerk, jnp.zeros((2, LANES), f32)], axis=0)
    odd = pltpu.roll(even, LANES - half // 2, 1)
    out = jnp.concatenate([even[0:6], odd[0:6], jnp.zeros((LANES - 12, LANES), f32)], axis=0).T
    for i in range(0, half // 2, 8):
        out_ref[pl.ds(i, 8), 0, :] = out[i : i + 8]


def finish_kernel(scale, in_ref, force_ref, jerk_ref):
    total = in_ref[0]
    for d in range(1, in_ref.shape[0]):
        total = total + in_ref[d]
    total = total * scale
    for slot in range(force_ref.shape[0]):
        force_ref[slot : slot + 1, :] = total[:, 6 * slot : 6 * slot + 3]
        jerk_ref[slot : slot + 1, :] = total[:, 6 * slot + 3 : 6 * slot + 6]


def near(x):
    return pltpu.with_memory_space_constraint(x, pltpu.VMEM)


def per_device(positions, velocities, masses, active_index):
    groups, members = lax.axis_size("grp"), lax.axis_size("dev")
    count = positions.shape[1]
    active = active_index.shape[0]
    f32 = jnp.float32
    packed = pl.pallas_call(
        pack_kernel,
        out_shape=pltpu.VMEM((groups, 8, count), f32),
        in_specs=[SCALARS, WHOLE, WHOLE, WHOLE],
        out_specs=WHOLE,
        name="pack",
    )(active_index, positions, velocities, masses.reshape(1, count))
    field = exchanged(packed, "grp", GRP_ORDER)
    spread = pl.pallas_call(
        spread_kernel,
        out_shape=pltpu.VMEM((members, 3, 1, LANES), f32),
        in_specs=[WHOLE],
        out_specs=WHOLE,
        name="spread",
    )(near(field))
    states = exchanged(spread, "dev", DEV_ORDER)
    per_group = active // groups
    partial = pl.pallas_call(
        pairs_kernel,
        out_shape=pltpu.VMEM((members, 1, LANES), f32),
        in_specs=[WHOLE, WHOLE],
        out_specs=WHOLE,
        name="pairs",
    )(near(states), near(field))
    arrived = exchanged(partial, "dev", DEV_ORDER)
    slots = per_group // members
    out = jax.ShapeDtypeStruct((slots, 3), f32)
    scale = 1.0 / (count * groups * members)
    force, jerk = pl.pallas_call(
        lambda *refs: finish_kernel(scale, *refs),
        out_shape=(out, out),
        in_specs=[WHOLE],
        out_specs=(WHOLE, WHOLE),
        name="finish",
    )(near(arrived))
    return force.T, jerk.T


def solution(mesh):
    both = ("grp", "dev")
    return jax.shard_map(
        per_device,
        mesh=mesh,
        in_specs=(P(None, both), P(None, both), P(both), P()),
        out_specs=(P(None, both), P(None, both)),
        check_vma=False,
    )
```

```python
import jax
import jax.numpy as jnp
from jax import lax
from jax.experimental import pallas as pl
from jax.experimental.pallas import tpu as pltpu
from jax.sharding import PartitionSpec as P

SOFT = 0.0025
LANES = 128
GRP_HEAD = (10, 0, 12, 3, 8, 2)
DEV_HEAD = (17,)
GRP_ORDER = GRP_HEAD + tuple(
    g for g in ((2 + i) % 4 * 4 + (2 + j) % 4 for j in range(4) for i in range(4)) if g not in GRP_HEAD
)
DEV_ORDER = DEV_HEAD + tuple(
    d for d in (2 * z + c for z in sorted(range(16), key=lambda z: min(z, 16 - z)) for c in (1, 0)) if d not in DEV_HEAD
)
WHOLE = pl.BlockSpec(memory_space=pltpu.VMEM)
SCALARS = pl.BlockSpec(memory_space=pltpu.SMEM)


def place_in(order, index):
    places = [order.index(i) for i in range(len(order))]
    words = [sum(p << 8 * n for n, p in enumerate(places[i : i + 4])) for i in range(0, len(places), 4)]
    word = jnp.int32(words[0])
    for i in range(1, len(words)):
        word = jnp.where(index >= 4 * i, words[i], word)
    return (word >> 8 * (index & 3)) & 255


def exchanged(x, axis, order):
    return lax.all_to_all(x, axis, 0, 0, axis_index_groups=[list(order)], tiled=True)


def pack_kernel(index_ref, pos_ref, vel_ref, mass_ref, out_ref):
    active = index_ref.shape[0]
    count = pos_ref.shape[1]
    groups = out_ref.shape[0]
    per_group = active // groups
    owner = lax.axis_index("grp") * lax.axis_size("dev") + lax.axis_index("dev")
    offset = owner * count
    mass = mass_ref[...]
    rows = jnp.concatenate([pos_ref[...], vel_ref[...], mass, jnp.zeros_like(mass)], axis=0)
    for g in range(groups):
        out_ref[g] = rows
    first = jnp.int32(0)
    step = active // 2
    while step:
        first = first + jnp.where(index_ref[first + (step - 1)] < offset, step, 0)
        step //= 2
    first = first + jnp.where(index_ref[first] < offset, 1, 0)
    lane = lax.broadcasted_iota(jnp.int32, (3, LANES), 1)
    rows = []
    for k in range(4):
        rank = jnp.minimum(first + k, active - 1)
        local = index_ref[rank] - offset
        held = (first + k < active) & (local < count)
        local = jnp.clip(local, 0, count - 1)
        chunk = pl.ds(pl.multiple_of(lax.div(local, LANES) * LANES, LANES), LANES)
        here = lane == lax.rem(local, LANES)
        pos = jnp.sum(jnp.where(here, pos_ref[:, chunk], 0.0), axis=1, keepdims=True)
        vel = jnp.sum(jnp.where(here, vel_ref[:, chunk], 0.0), axis=1, keepdims=True)
        slot = lax.rem(rank, per_group)
        slot = (slot & 1) * (per_group // 2) + place_in(DEV_ORDER, slot >> 1)
        slot = jnp.where(held, slot, LANES)
        state = jnp.where(lane == slot, pos, jnp.where(lane == slot + LANES // 2, vel, 0.0))
        rows.append((place_in(GRP_ORDER, lax.div(rank, per_group)), state))
    for row, state in rows:
        for c in range(3):
            tile = pl.ds(c * LANES, LANES)
            out_ref[row, 7:8, tile] = out_ref[row, 7:8, tile] + state[c : c + 1]


def spread_kernel(in_ref, out_ref):
    for c in range(3):
        tile = pl.ds(c * LANES, LANES)
        total = in_ref[0, 7:8, tile]
        for g in range(1, in_ref.shape[0]):
            total = total + in_ref[g, 7:8, tile]
        for d in range(out_ref.shape[0]):
            out_ref[d, c] = total


def in_parts(x, count):
    parts = []
    for _ in range(count):
        parts.append(x.astype(jnp.bfloat16).astype(jnp.float32))
        x = x - parts[-1]
    return parts


def pairs_kernel(state_ref, field_ref, out_ref):
    sources, _, count = field_ref.shape
    half = LANES // 2
    f32, bf16 = jnp.float32, jnp.bfloat16
    rows = []
    for c in range(3):
        total = state_ref[0, c]
        for d in range(1, state_ref.shape[0]):
            total = total + state_ref[d, c]
        rows.append(total)
    state = jnp.concatenate(rows + [jnp.zeros((5, LANES), f32)], axis=0)
    packed = state.T
    actives = [
        [jnp.broadcast_to(packed[h + g : h + g + 8, c : c + 1], (8, LANES)) for h in (0, half) for c in range(3)]
        for g in range(0, half, 8)
    ]
    pos0, vel0 = state[0:3, 0:1], state[0:3, half : half + 1]
    origin = jnp.concatenate([pos0, vel0, jnp.zeros((2, 1), f32)], axis=0)
    row = lax.broadcasted_iota(jnp.int32, (8, count), 0)
    step = 2 * LANES

    def one_source(b, sums):
        stars = field_ref[b] - origin
        stars = jnp.where(row == 6, stars, stars * field_ref[b, 6:7, :])
        high, middle, low = in_parts(stars, 3)
        stars = jnp.concatenate(
            [
                jnp.concatenate([high, middle], axis=0).astype(bf16),
                jnp.concatenate([low, jnp.zeros_like(low)], axis=0).astype(bf16),
            ],
            axis=0,
        )
        for start in range(0, count, step):
            weights, ratios = [], []
            for t in range(start, start + step, LANES):
                star = [jnp.broadcast_to(field_ref[b, c : c + 1, t : t + LANES], (8, LANES)) for c in range(6)]
                column_w, column_r = [], []
                for act in actives:
                    dx = [star[c] - act[c] for c in range(3)]
                    dv = [star[3 + c] - act[3 + c] for c in range(3)]
                    r2 = dx[0] * dx[0] + dx[1] * dx[1] + dx[2] * dx[2] + SOFT
                    inv = lax.rsqrt(r2)
                    rv = dx[0] * dv[0] + dx[1] * dv[1] + dx[2] * dv[2]
                    inv2 = inv * inv
                    weight = inv * inv2
                    column_w.append(weight)
                    column_r.append(rv * inv2 * weight)
                weights.append(jnp.concatenate(column_w, axis=0))
                ratios.append(jnp.concatenate(column_r, axis=0))
            parts = in_parts(jnp.concatenate(weights, axis=1), 2) + in_parts(jnp.concatenate(ratios, axis=1), 2)
            sums = sums + lax.dot_general(
                stars[:, start : start + step],
                jnp.concatenate([p.astype(bf16) for p in parts], axis=0),
                (((1,), (1,)), ((), ())),
                preferred_element_type=f32,
            )
        return sums

    sums = jnp.zeros((32, 4 * half), f32)
    for b in range(sources):
        sums = one_source(b, sums)
    sums = sums[0:8] + sums[8:16] + sums[16:24]
    by_weight, by_ratio = sums[:, :LANES], sums[:, LANES:]
    by_weight = by_weight + pltpu.roll(by_weight, half, 1)
    by_ratio = by_ratio + pltpu.roll(by_ratio, half, 1)
    pos = state[0:3] - pos0
    vel = pltpu.roll(state, half, 1)[0:3] - vel0
    force = by_weight[0:3] - pos * by_weight[6:7]
    jerk = by_weight[3:6] - vel * by_weight[6:7] - 3.0 * (by_ratio[0:3] - pos * by_ratio[6:7])
    even = jnp.concatenate([force, jerk, jnp.zeros((2, LANES), f32)], axis=0)
    odd = pltpu.roll(even, LANES - half // 2, 1)
    out = jnp.concatenate([even[0:6], odd[0:6], jnp.zeros((LANES - 12, LANES), f32)], axis=0).T
    for i in range(0, half // 2, 8):
        out_ref[pl.ds(i, 8), 0, :] = out[i : i + 8]


def finish_kernel(scale, in_ref, force_ref, jerk_ref):
    total = in_ref[0]
    for d in range(1, in_ref.shape[0]):
        total = total + in_ref[d]
    total = total * scale
    for slot in range(force_ref.shape[0]):
        force_ref[slot : slot + 1, :] = total[:, 6 * slot : 6 * slot + 3]
        jerk_ref[slot : slot + 1, :] = total[:, 6 * slot + 3 : 6 * slot + 6]


def near(x):
    return pltpu.with_memory_space_constraint(x, pltpu.VMEM)


def per_device(positions, velocities, masses, active_index):
    groups, members = lax.axis_size("grp"), lax.axis_size("dev")
    count = positions.shape[1]
    active = active_index.shape[0]
    f32 = jnp.float32
    packed = pl.pallas_call(
        pack_kernel,
        out_shape=pltpu.VMEM((groups, 8, count), f32),
        in_specs=[SCALARS, WHOLE, WHOLE, WHOLE],
        out_specs=WHOLE,
        name="pack",
    )(active_index, positions, velocities, masses.reshape(1, count))
    field = exchanged(packed, "grp", GRP_ORDER)
    spread = pl.pallas_call(
        spread_kernel,
        out_shape=pltpu.VMEM((members, 3, 1, LANES), f32),
        in_specs=[WHOLE],
        out_specs=WHOLE,
        name="spread",
    )(near(field))
    states = exchanged(spread, "dev", DEV_ORDER)
    per_group = active // groups
    partial = pl.pallas_call(
        pairs_kernel,
        out_shape=pltpu.VMEM((members, 1, LANES), f32),
        in_specs=[WHOLE, WHOLE],
        out_specs=WHOLE,
        name="pairs",
    )(near(states), near(field))
    arrived = exchanged(partial, "dev", DEV_ORDER)
    slots = per_group // members
    out = jax.ShapeDtypeStruct((slots, 3), f32)
    scale = 1.0 / (count * groups * members)
    force, jerk = pl.pallas_call(
        lambda *refs: finish_kernel(scale, *refs),
        out_shape=(out, out),
        in_specs=[WHOLE],
        out_specs=(WHOLE, WHOLE),
        name="finish",
    )(near(arrived))
    return force.T, jerk.T


def solution(mesh):
    both = ("grp", "dev")
    return jax.shard_map(
        per_device,
        mesh=mesh,
        in_specs=(P(None, both), P(None, both), P(both), P()),
        out_specs=(P(None, both), P(None, both)),
        check_vma=False,
    )
```

```python
import jax
import jax.numpy as jnp
from jax import lax
from jax.experimental import pallas as pl
from jax.experimental.pallas import tpu as pltpu
from jax.sharding import PartitionSpec as P

SOFT = 0.0025
LANES = 128
GRP_HEAD = (10, 0, 12, 3, 8, 2)
DEV_HEAD = (17, 1, 0, 16)
GRP_ORDER = GRP_HEAD + tuple(
    g for g in ((2 + i) % 4 * 4 + (2 + j) % 4 for j in range(4) for i in range(4)) if g not in GRP_HEAD
)
DEV_ORDER = DEV_HEAD + tuple(
    d for d in (2 * z + c for z in sorted(range(16), key=lambda z: min(z, 16 - z)) for c in (1, 0)) if d not in DEV_HEAD
)
WHOLE = pl.BlockSpec(memory_space=pltpu.VMEM)
SCALARS = pl.BlockSpec(memory_space=pltpu.SMEM)


def place_in(order, index):
    places = [order.index(i) for i in range(len(order))]
    words = [sum(p << 8 * n for n, p in enumerate(places[i : i + 4])) for i in range(0, len(places), 4)]
    word = jnp.int32(words[0])
    for i in range(1, len(words)):
        word = jnp.where(index >= 4 * i, words[i], word)
    return (word >> 8 * (index & 3)) & 255


def exchanged(x, axis, order):
    return lax.all_to_all(x, axis, 0, 0, axis_index_groups=[list(order)], tiled=True)


def pack_kernel(index_ref, pos_ref, vel_ref, mass_ref, out_ref):
    active = index_ref.shape[0]
    count = pos_ref.shape[1]
    groups = out_ref.shape[0]
    per_group = active // groups
    owner = lax.axis_index("grp") * lax.axis_size("dev") + lax.axis_index("dev")
    offset = owner * count
    mass = mass_ref[...]
    rows = jnp.concatenate([pos_ref[...], vel_ref[...], mass, jnp.zeros_like(mass)], axis=0)
    for g in range(groups):
        out_ref[g] = rows
    first = jnp.int32(0)
    step = active // 2
    while step:
        first = first + jnp.where(index_ref[first + (step - 1)] < offset, step, 0)
        step //= 2
    first = first + jnp.where(index_ref[first] < offset, 1, 0)
    lane = lax.broadcasted_iota(jnp.int32, (3, LANES), 1)
    rows = []
    for k in range(4):
        rank = jnp.minimum(first + k, active - 1)
        local = index_ref[rank] - offset
        held = (first + k < active) & (local < count)
        local = jnp.clip(local, 0, count - 1)
        chunk = pl.ds(pl.multiple_of(lax.div(local, LANES) * LANES, LANES), LANES)
        here = lane == lax.rem(local, LANES)
        pos = jnp.sum(jnp.where(here, pos_ref[:, chunk], 0.0), axis=1, keepdims=True)
        vel = jnp.sum(jnp.where(here, vel_ref[:, chunk], 0.0), axis=1, keepdims=True)
        slot = lax.rem(rank, per_group)
        slot = (slot & 1) * (per_group // 2) + place_in(DEV_ORDER, slot >> 1)
        slot = jnp.where(held, slot, LANES)
        state = jnp.where(lane == slot, pos, jnp.where(lane == slot + LANES // 2, vel, 0.0))
        rows.append((place_in(GRP_ORDER, lax.div(rank, per_group)), state))
    for row, state in rows:
        for c in range(3):
            tile = pl.ds(c * LANES, LANES)
            out_ref[row, 7:8, tile] = out_ref[row, 7:8, tile] + state[c : c + 1]


def spread_kernel(in_ref, out_ref):
    for c in range(3):
        tile = pl.ds(c * LANES, LANES)
        total = in_ref[0, 7:8, tile]
        for g in range(1, in_ref.shape[0]):
            total = total + in_ref[g, 7:8, tile]
        for d in range(out_ref.shape[0]):
            out_ref[d, c] = total


def in_parts(x, count):
    parts = []
    for _ in range(count):
        parts.append(x.astype(jnp.bfloat16).astype(jnp.float32))
        x = x - parts[-1]
    return parts


def pairs_kernel(state_ref, field_ref, out_ref):
    sources, _, count = field_ref.shape
    half = LANES // 2
    f32, bf16 = jnp.float32, jnp.bfloat16
    rows = []
    for c in range(3):
        total = state_ref[0, c]
        for d in range(1, state_ref.shape[0]):
            total = total + state_ref[d, c]
        rows.append(total)
    state = jnp.concatenate(rows + [jnp.zeros((5, LANES), f32)], axis=0)
    packed = state.T
    actives = [
        [jnp.broadcast_to(packed[h + g : h + g + 8, c : c + 1], (8, LANES)) for h in (0, half) for c in range(3)]
        for g in range(0, half, 8)
    ]
    pos0, vel0 = state[0:3, 0:1], state[0:3, half : half + 1]
    origin = jnp.concatenate([pos0, vel0, jnp.zeros((2, 1), f32)], axis=0)
    row = lax.broadcasted_iota(jnp.int32, (8, count), 0)
    step = 2 * LANES

    def one_source(b, sums):
        stars = field_ref[b] - origin
        stars = jnp.where(row == 6, stars, stars * field_ref[b, 6:7, :])
        high, middle, low = in_parts(stars, 3)
        stars = jnp.concatenate(
            [
                jnp.concatenate([high, middle], axis=0).astype(bf16),
                jnp.concatenate([low, jnp.zeros_like(low)], axis=0).astype(bf16),
            ],
            axis=0,
        )
        for start in range(0, count, step):
            weights, ratios = [], []
            for t in range(start, start + step, LANES):
                star = [jnp.broadcast_to(field_ref[b, c : c + 1, t : t + LANES], (8, LANES)) for c in range(6)]
                column_w, column_r = [], []
                for act in actives:
                    dx = [star[c] - act[c] for c in range(3)]
                    dv = [star[3 + c] - act[3 + c] for c in range(3)]
                    r2 = dx[0] * dx[0] + dx[1] * dx[1] + dx[2] * dx[2] + SOFT
                    inv = lax.rsqrt(r2)
                    rv = dx[0] * dv[0] + dx[1] * dv[1] + dx[2] * dv[2]
                    inv2 = inv * inv
                    weight = inv * inv2
                    column_w.append(weight)
                    column_r.append(rv * inv2 * weight)
                weights.append(jnp.concatenate(column_w, axis=0))
                ratios.append(jnp.concatenate(column_r, axis=0))
            parts = in_parts(jnp.concatenate(weights, axis=1), 2) + in_parts(jnp.concatenate(ratios, axis=1), 2)
            sums = sums + lax.dot_general(
                stars[:, start : start + step],
                jnp.concatenate([p.astype(bf16) for p in parts], axis=0),
                (((1,), (1,)), ((), ())),
                preferred_element_type=f32,
            )
        return sums

    sums = jnp.zeros((32, 4 * half), f32)
    for b in range(sources):
        sums = one_source(b, sums)
    sums = sums[0:8] + sums[8:16] + sums[16:24]
    by_weight, by_ratio = sums[:, :LANES], sums[:, LANES:]
    by_weight = by_weight + pltpu.roll(by_weight, half, 1)
    by_ratio = by_ratio + pltpu.roll(by_ratio, half, 1)
    pos = state[0:3] - pos0
    vel = pltpu.roll(state, half, 1)[0:3] - vel0
    force = by_weight[0:3] - pos * by_weight[6:7]
    jerk = by_weight[3:6] - vel * by_weight[6:7] - 3.0 * (by_ratio[0:3] - pos * by_ratio[6:7])
    even = jnp.concatenate([force, jerk, jnp.zeros((2, LANES), f32)], axis=0)
    odd = pltpu.roll(even, LANES - half // 2, 1)
    out = jnp.concatenate([even[0:6], odd[0:6], jnp.zeros((LANES - 12, LANES), f32)], axis=0).T
    for i in range(0, half // 2, 8):
        out_ref[pl.ds(i, 8), 0, :] = out[i : i + 8]


def finish_kernel(scale, in_ref, force_ref, jerk_ref):
    total = in_ref[0]
    for d in range(1, in_ref.shape[0]):
        total = total + in_ref[d]
    total = total * scale
    for slot in range(force_ref.shape[0]):
        force_ref[slot : slot + 1, :] = total[:, 6 * slot : 6 * slot + 3]
        jerk_ref[slot : slot + 1, :] = total[:, 6 * slot + 3 : 6 * slot + 6]


def near(x):
    return pltpu.with_memory_space_constraint(x, pltpu.VMEM)


def per_device(positions, velocities, masses, active_index):
    groups, members = lax.axis_size("grp"), lax.axis_size("dev")
    count = positions.shape[1]
    active = active_index.shape[0]
    f32 = jnp.float32
    packed = pl.pallas_call(
        pack_kernel,
        out_shape=pltpu.VMEM((groups, 8, count), f32),
        in_specs=[SCALARS, WHOLE, WHOLE, WHOLE],
        out_specs=WHOLE,
        name="pack",
    )(active_index, positions, velocities, masses.reshape(1, count))
    field = exchanged(packed, "grp", GRP_ORDER)
    spread = pl.pallas_call(
        spread_kernel,
        out_shape=pltpu.VMEM((members, 3, 1, LANES), f32),
        in_specs=[WHOLE],
        out_specs=WHOLE,
        name="spread",
    )(near(field))
    states = exchanged(spread, "dev", DEV_ORDER)
    per_group = active // groups
    partial = pl.pallas_call(
        pairs_kernel,
        out_shape=pltpu.VMEM((members, 1, LANES), f32),
        in_specs=[WHOLE, WHOLE],
        out_specs=WHOLE,
        name="pairs",
    )(near(states), near(field))
    arrived = exchanged(partial, "dev", DEV_ORDER)
    slots = per_group // members
    out = jax.ShapeDtypeStruct((slots, 3), f32)
    scale = 1.0 / (count * groups * members)
    force, jerk = pl.pallas_call(
        lambda *refs: finish_kernel(scale, *refs),
        out_shape=(out, out),
        in_specs=[WHOLE],
        out_specs=(WHOLE, WHOLE),
        name="finish",
    )(near(arrived))
    return force.T, jerk.T


def solution(mesh):
    both = ("grp", "dev")
    return jax.shard_map(
        per_device,
        mesh=mesh,
        in_specs=(P(None, both), P(None, both), P(both), P()),
        out_specs=(P(None, both), P(None, both)),
        check_vma=False,
    )
```
